32 devices in a mesh: ctx: 16 (over z, y, x), tp: 2 (over core).
Axes of the slice: x: 2, y: 2, z: 4, core: 2. Of those that a mesh axis runs over, the one named last changes fastest.
Arguments:
- tokens: bfloat16 [8192, 8192], P('ctx', 'tp'), may hold values from -18 to 18
- w_query: bfloat16 [8192, 8192], P('ctx', 'tp'), may hold values from -0.0625 to 0.0625
- key_weight: bfloat16 [8192, 1024], P('ctx', 'tp'), may hold values from -0.0625 to 0.0625
- value_weight: bfloat16 [8192, 1024], P('ctx', 'tp'), may hold values from -0.0625 to 0.0625
- prefix_cache_blocks: bfloat16 [8, 128, 2, 128, 128], P('tp', 'ctx'), may hold values from -6 to 6
- selected_owner: int32 [8, 64, 8], P('tp', 'ctx'), may hold values from 0 to 15, all different within a row; in each aligned block of 4 rows (0 to 3, 4 to 7, ..., all dimensions but the last counted through in order) at most 3 rows name the same one
- selected_offset: int32 [8, 64, 8], P('tp', 'ctx'), may hold values from 0 to 7
- selected_alive_mask: int32 [8, 64, 8], P('tp', 'ctx'), may hold values 0 or 1
Outputs:
- attended: bfloat16 [8192, 8192], P('ctx', 'tp')
The draws below stay inside these ranges and needn't reach their ends.
Inputs may be any that keep to these rules, and one draw needn't show every extreme that they name: `selected_owner`: each row names 8 different indices of ctx. In the rows of one device (aligned runs of 4 query blocks of one head) no index is named more than 3 times.
All inputs are finite; a program needn't handle non-finite values. No bound on the sum of `selected_alive_mask` on one device may be relied on, other than what follows from the above.
Results may differ from the reference program's by a relative error of at most 0.017.
Values may be sent and summed in bfloat16 or wider, within the bound.
No kernel may reach another device: no remote copies, remote signals or barrier semaphores. Data moves between devices by JAX's collectives and lax.ppermute only.
A program may use at most 192 MiB of HBM per device.

```python
import math
import jax
import jax.numpy as jnp
import numpy as np
from jax import lax

MODEL_WIDTH = 8192
QUERY_HEADS = 64
KEY_HEADS = 8
HEAD_SIZE = 128
BLOCK_TOKENS = 128
SELECTED_BLOCKS = 8
QUERY_PER_SHARD = 4
CACHED_PER_SHARD = 8
SPAN_TOKENS = 8192
QUERY_BLOCKS = 64
CACHED_BLOCKS = 128
SELECT_LIMIT = 3
N_CTX = 16


def draw_tokens(key, part):
    key = jax.random.fold_in(key, 7)
    return jnp.clip(jax.random.normal(key, (SPAN_TOKENS, MODEL_WIDTH), jnp.float32), -6.0, 6.0).astype(jnp.bfloat16)


def with_ends(drawn, key, smallest, high):
    shape = drawn.shape
    index_at = [jax.random.randint(jax.random.fold_in(key, axis), (), 0, shape[axis]) for axis in range(len(shape))]
    drawn = drawn.at[tuple(index_at)].set(smallest)
    longest = shape.index(max(shape))
    index_at[longest] = (index_at[longest] + 1) % shape[longest]
    return drawn.at[tuple(index_at)].set(high)


def levels(stream_key, shape, shards, smallest, top_value):
    loudness = 1.0
    for position, shards_of in shards:
        steps = jax.random.uniform(jax.random.fold_in(jax.random.fold_in(stream_key, 6), position), (shards_of,), jnp.float32, smallest / len(shards), top_value / len(shards))
        loudness = loudness * jnp.repeat(jnp.exp(steps), shape[position] // shards_of).reshape((-1,) + (1,) * (len(shape) - 1 - position))
    return loudness


def assign_block(key, own, number, rows, number_of, top, reach, skew):
    ranking = jax.random.permutation(key, number_of)
    crowded, usual = shares(number_of, rows * top, reach, skew, True), shares(number_of, rows * top, reach, skew, False)
    places = jnp.arange(number_of)

    def named(lengths, offset_by):
        used = int((lengths > 0).sum())
        fixed = max(1, used // 4)
        passed = fixed + (places - fixed + offset_by * (used - fixed)) % max(1, number_of - fixed)
        return jnp.zeros((number_of,), jnp.int32).at[ranking[jnp.where(places < fixed, places, passed)]].set(jnp.asarray(lengths, jnp.int32))

    lengths = jnp.where(number % 4 == 0, named(crowded, number // 4), named(usual, number - number // 4 - 1))
    mixed = jax.random.permutation(jax.random.fold_in(own, 3), number_of)
    source_of, sink = mixed[0:number_of // 2 * 2:2], mixed[1:number_of // 2 * 2:2]
    room = jnp.minimum(lengths[source_of] - 1, reach - lengths[sink]) // 2
    room = jnp.where((source_of == ranking[0]) | (sink == ranking[0]) | (lengths[sink] == 0), 0, jnp.maximum(room, 0))
    passed = jax.random.randint(jax.random.fold_in(own, 4), (number_of // 2,), 0, 1 << 20) % (room + 1)
    lengths = lengths.at[source_of].add(-passed).at[sink].add(passed)
    items = jnp.searchsorted(jnp.cumsum(lengths), jnp.arange(rows * top), side="right").astype(jnp.int32)
    grid = items.reshape(top, rows).T
    grid = grid[jax.random.permutation(jax.random.fold_in(own, 1), rows)]
    offset_by = jax.random.randint(jax.random.fold_in(own, 2), (rows, 1), 0, top)
    return jnp.take_along_axis(grid, (jnp.arange(top)[None, :] + offset_by) % top, axis=1)


def shares(count, total, reach, lean, full):
    weights = [(1 << 20) // math.isqrt(rank ** lean) + 1 for rank in range(1, count + 1)]
    largest = reach if full else min(reach, max(-(-total // count), total * weights[0] // sum(weights)))
    least = 1 if total - largest >= count - 1 else 0
    given, rest = [largest] + [least] * (count - 1), total - largest - least * (count - 1)
    while rest > 0:
        candidates = [i for i in range(1, count) if given[i] < largest] or [i for i in range(1, count) if given[i] < reach]
        pool, remaining = sum([weights[i] for i in candidates]), rest
        for i in candidates:
            extra = min(reach - given[i], max(1, remaining * weights[i] // pool), rest)
            given[i] = given[i] + extra
            rest = rest - extra
    return np.array(given)


def centred(rng, shape, deviation, bound, cuts=(), kind=jnp.bfloat16):
    array = jax.random.normal(rng, shape, jnp.float32) * deviation
    if len(cuts) > 0:
        array = levels(rng, shape, cuts, -0.22, 0.18) * array
    return jnp.clip(array, min=-bound, max=bound).astype(kind)


def setup_inputs(seed: int = 0) -> dict:
    key_list = jax.random.split(jax.random.key(seed), 9)
    tokens = draw_tokens(jax.random.fold_in(key_list[8], 71), 0)
    w_query = centred(key_list[1], (MODEL_WIDTH, QUERY_HEADS * HEAD_SIZE), MODEL_WIDTH ** -0.5, 0.0625, ((0, 16), (1, 2)))
    key_weight = centred(key_list[2], (MODEL_WIDTH, KEY_HEADS * HEAD_SIZE), MODEL_WIDTH ** -0.5, 0.0625, ((0, 16), (1, 2)))
    value_weight = centred(key_list[3], (MODEL_WIDTH, KEY_HEADS * HEAD_SIZE), MODEL_WIDTH ** -0.5, 0.0625, ((0, 16), (1, 2)))
    prefix_cache_blocks = centred(key_list[4], (KEY_HEADS, CACHED_BLOCKS, 2, BLOCK_TOKENS, HEAD_SIZE), 1.0, 6.0, ((0, 2), (1, 16)))
    selected_owner_keys = jax.random.split(jax.random.fold_in(key_list[5], 1), KEY_HEADS * QUERY_BLOCKS // QUERY_PER_SHARD)
    selected_owner_turns = jax.random.permutation(jax.random.fold_in(key_list[5], 3), KEY_HEADS * QUERY_BLOCKS // QUERY_PER_SHARD)
    selected_owner = jax.vmap(lambda own, number: assign_block(jax.random.fold_in(key_list[5], 2), own, number, QUERY_PER_SHARD, N_CTX, SELECTED_BLOCKS, SELECT_LIMIT, 2))(selected_owner_keys, selected_owner_turns).reshape((KEY_HEADS, QUERY_BLOCKS, SELECTED_BLOCKS))
    selected_offset = with_ends(jax.random.randint(key_list[6], (KEY_HEADS, QUERY_BLOCKS, SELECTED_BLOCKS), 0, CACHED_PER_SHARD), jax.random.fold_in(key_list[6], 1), 0, CACHED_PER_SHARD - 1).astype(jnp.int32)
    selected_alive_mask = with_ends((jax.random.randint(key_list[7], (KEY_HEADS, QUERY_BLOCKS, SELECTED_BLOCKS), 0, 4) < 3).astype(jnp.int32), jax.random.fold_in(key_list[7], 1), 0, 1)
    return {"tokens": tokens, "w_query": w_query, "key_weight": key_weight, "value_weight": value_weight, "prefix_cache_blocks": prefix_cache_blocks, "selected_owner": selected_owner, "selected_offset": selected_offset, "selected_alive_mask": selected_alive_mask}


rope_base = 500000.0
neg_fill = -1e+30

def apply_rotation(values, token_positions):
    half_dim = values.shape[-1] // 2
    steps = jnp.arange(half_dim).astype(jnp.float32)
    inverse = jnp.power(jnp.float32(rope_base), -2.0 * steps / values.shape[-1])
    angle = token_positions.astype(jnp.float32)[:, None] * inverse[None, :]
    cosine = jnp.cos(angle)[:, None, :]
    sine_part = jnp.sin(angle)[:, None, :]
    lower_half = values[..., :half_dim]
    upper_half = values[..., half_dim:]
    return jnp.concatenate([lower_half * cosine - upper_half * sine_part, upper_half * cosine + lower_half * sine_part], axis=-1)

def attend(query, selected, live_slots, own_keys, own_values):
    scaling = 1.0 / jnp.sqrt(jnp.float32(query.shape[-1]))
    query_wide = query.astype(jnp.float32)
    far_keys = selected[:, :, :, 0].astype(jnp.float32)
    far_values = selected[:, :, :, 1].astype(jnp.float32)
    far_scores = jnp.einsum('bihgd,hbskd->bhgisk', query_wide, far_keys) * scaling
    alive = jnp.transpose(live_slots, (1, 0, 2))[:, :, None, None, :, None] > 0
    far_scores = jnp.where(alive, far_scores, neg_fill)
    near_scores = jnp.einsum('bihgd,bjhd->bhgij', query_wide, own_keys.astype(jnp.float32)) * scaling
    row_ids = jnp.arange(query.shape[1])
    causal = row_ids[:, None] >= row_ids[None, :]
    near_scores = jnp.where(causal, near_scores, neg_fill)
    row_max = jnp.maximum(lax.optimization_barrier(jnp.max(far_scores, axis=(4, 5))), lax.optimization_barrier(jnp.max(near_scores, axis=4)))
    far_exp = jnp.exp(far_scores - row_max[..., None, None])
    near_exp = jnp.exp(near_scores - row_max[..., None])
    denominator = lax.optimization_barrier(jnp.sum(far_exp, axis=(4, 5))) + lax.optimization_barrier(jnp.sum(near_exp, axis=4))
    far_prob = (far_exp / denominator[..., None, None]).astype(jnp.bfloat16)
    near_prob = (near_exp / denominator[..., None]).astype(jnp.bfloat16)
    mixed = jnp.einsum('bhgisk,hbskd->bihgd', far_prob.astype(jnp.float32), far_values)
    mixed = mixed + jnp.einsum('bhgij,bjhd->bihgd', near_prob.astype(jnp.float32), own_values.astype(jnp.float32))
    return mixed

def reference(tokens, w_query, key_weight, value_weight, prefix_cache_blocks, selected_owner, selected_offset, selected_alive_mask):
    query_proj = jnp.dot(tokens, w_query, preferred_element_type=jnp.float32)
    key_projected = jnp.dot(tokens, key_weight, preferred_element_type=jnp.float32)
    value_projected = jnp.dot(tokens, value_weight, preferred_element_type=jnp.float32)
    token_positions = CACHED_BLOCKS * BLOCK_TOKENS + jnp.arange(SPAN_TOKENS, dtype=jnp.int32)
    rotated_queries = apply_rotation(query_proj.reshape(SPAN_TOKENS, QUERY_HEADS, HEAD_SIZE), token_positions).astype(jnp.bfloat16)
    rotated_keys = apply_rotation(key_projected.reshape(SPAN_TOKENS, KEY_HEADS, HEAD_SIZE), token_positions).astype(jnp.bfloat16)
    fresh_values = value_projected.astype(jnp.bfloat16).reshape(SPAN_TOKENS, KEY_HEADS, HEAD_SIZE)
    query_group_width = QUERY_HEADS // KEY_HEADS
    query_block_rows = rotated_queries.reshape(QUERY_BLOCKS, BLOCK_TOKENS, KEY_HEADS, query_group_width, HEAD_SIZE)
    key_block_rows = rotated_keys.reshape(QUERY_BLOCKS, BLOCK_TOKENS, KEY_HEADS, HEAD_SIZE)
    value_block_rows = fresh_values.reshape(QUERY_BLOCKS, BLOCK_TOKENS, KEY_HEADS, HEAD_SIZE)
    block_rows = selected_owner * CACHED_PER_SHARD + selected_offset

    def one_block(index):
        chosen = lax.dynamic_index_in_dim(block_rows, index, axis=1, keepdims=False)
        live_slots = lax.dynamic_index_in_dim(selected_alive_mask, index, axis=1, keepdims=True)
        picked = jax.vmap(lambda cache_table, wanted: jnp.take(cache_table, wanted, axis=0))(prefix_cache_blocks, chosen)
        query = lax.dynamic_index_in_dim(query_block_rows, index, axis=0, keepdims=True)
        own_keys = lax.dynamic_index_in_dim(key_block_rows, index, axis=0, keepdims=True)
        own_values = lax.dynamic_index_in_dim(value_block_rows, index, axis=0, keepdims=True)
        result = attend(query, picked[:, None], live_slots, own_keys, own_values)
        return result[0].astype(jnp.bfloat16)
    outputs = lax.map(one_block, jnp.arange(QUERY_BLOCKS, dtype=jnp.int32))
    return outputs.reshape(SPAN_TOKENS, QUERY_HEADS * HEAD_SIZE)
```

```python
import functools

import jax
import jax.numpy as jnp
from jax import lax
from jax.experimental import pallas as pl
from jax.experimental.pallas import tpu as pltpu
from jax.sharding import PartitionSpec as P

rope_base = 500000.0
neg_fill = -1e30


def apply_rotation(values, token_positions):
    half_dim = values.shape[-1] // 2
    steps = jnp.arange(half_dim).astype(jnp.float32)
    inverse = jnp.power(jnp.float32(rope_base), -2.0 * steps / values.shape[-1])
    angle = token_positions.astype(jnp.float32)[:, None] * inverse[None, :]
    cosine = jnp.cos(angle)[:, None, :]
    sine_part = jnp.sin(angle)[:, None, :]
    lower_half = values[..., :half_dim]
    upper_half = values[..., half_dim:]
    return jnp.concatenate(
        [
            lower_half * cosine - upper_half * sine_part,
            upper_half * cosine + lower_half * sine_part,
        ],
        axis=-1,
    )


def attend(query, selected, live_slots, own_keys, own_values):
    scaling = 1.0 / jnp.sqrt(jnp.float32(query.shape[-1]))
    far_scores = (
        jnp.einsum(
            "bihgd,hbskd->bhgisk", query, selected[:, :, :, 0], preferred_element_type=jnp.float32
        )
        * scaling
    )
    alive = jnp.transpose(live_slots, (1, 0, 2))[:, :, None, None, :, None] > 0
    far_scores = jnp.where(alive, far_scores, neg_fill)
    near_scores = (
        jnp.einsum("bihgd,bjhd->bhgij", query, own_keys, preferred_element_type=jnp.float32)
        * scaling
    )
    row_ids = jnp.arange(query.shape[1])
    causal = row_ids[:, None] >= row_ids[None, :]
    near_scores = jnp.where(causal, near_scores, neg_fill)
    row_max = jnp.maximum(jnp.max(far_scores, axis=(4, 5)), jnp.max(near_scores, axis=4))
    far_exp = jnp.exp(far_scores - row_max[..., None, None])
    near_exp = jnp.exp(near_scores - row_max[..., None])
    denominator = jnp.sum(far_exp, axis=(4, 5)) + jnp.sum(near_exp, axis=4)
    far_prob = (far_exp / denominator[..., None, None]).astype(jnp.bfloat16)
    near_prob = (near_exp / denominator[..., None]).astype(jnp.bfloat16)
    mixed = jnp.einsum(
        "bhgisk,hbskd->bihgd", far_prob, selected[:, :, :, 1], preferred_element_type=jnp.float32
    )
    mixed = mixed + jnp.einsum(
        "bhgij,bjhd->bihgd", near_prob, own_values, preferred_element_type=jnp.float32
    )
    return mixed


def per_device(
    tokens,
    w_query,
    key_weight,
    value_weight,
    prefix_cache_blocks,
    selected_owner,
    selected_offset,
    selected_alive_mask,
):
    tok_rows = tokens.shape[0]
    ctx_devices = lax.axis_size("ctx")
    kv_heads = prefix_cache_blocks.shape[0]
    blocks_dev = prefix_cache_blocks.shape[1]
    block_len = prefix_cache_blocks.shape[3]
    head_dim = prefix_cache_blocks.shape[4]
    query_blocks = selected_owner.shape[1]
    selections = selected_owner.shape[2]
    query_heads = w_query.shape[1] // head_dim
    query_group_width = query_heads // kv_heads
    capacity = min(query_blocks, (query_blocks * selections + ctx_devices - 1) // ctx_devices + 1)
    gathered = lax.all_gather(tokens, "tp", axis=1, tiled=True)
    pieces = (
        lax.all_gather(w_query, "ctx", axis=0, tiled=True),
        lax.all_gather(key_weight, "ctx", axis=0, tiled=True),
        lax.all_gather(value_weight, "ctx", axis=0, tiled=True),
    )
    query_proj, key_projected, value_projected = tuple(
        (jnp.dot(gathered, shard_rows, preferred_element_type=jnp.float32) for shard_rows in pieces)
    )
    requests = query_blocks * selections
    owners = selected_owner.reshape(kv_heads, requests)
    offsets = selected_offset.reshape(kv_heads, requests)
    owner_hot = (owners[:, :, None] == jnp.arange(ctx_devices, dtype=jnp.int32)).astype(jnp.int32)
    earlier = jnp.cumsum(owner_hot, axis=1) - owner_hot
    ordinal = jnp.sum(earlier * owner_hot, axis=2)
    slot_count = kv_heads * capacity
    slot_index = jnp.arange(kv_heads, dtype=jnp.int32)[:, None] * capacity + ordinal
    slot_hot = (slot_index[:, :, None] == jnp.arange(slot_count, dtype=jnp.int32)).astype(jnp.int32)
    entries = jnp.arange(kv_heads, dtype=jnp.int32)[:, None] * blocks_dev + offsets
    outgoing = jnp.einsum("hrn,hrs->ns", owner_hot * entries[:, :, None], slot_hot)
    cache_table = prefix_cache_blocks.reshape(kv_heads * blocks_dev, 2, block_len, head_dim)
    found_blocks = jnp.take(
        cache_table,
        lax.all_to_all(outgoing, "ctx", split_axis=0, concat_axis=0, tiled=True),
        axis=0,
    )
    arrived = lax.all_to_all(found_blocks, "ctx", split_axis=0, concat_axis=0, tiled=True)
    flattened = arrived.reshape(ctx_devices * slot_count, 2, block_len, head_dim)
    locator = owners * slot_count + slot_index
    picked = jnp.take(flattened, locator.reshape(-1), axis=0)
    selected = picked.reshape(kv_heads, query_blocks, selections, 2, block_len, head_dim)
    token_positions = (
        blocks_dev * ctx_devices * block_len
        + lax.axis_index("ctx") * tok_rows
        + jnp.arange(tok_rows, dtype=jnp.int32)
    )
    rotated_queries = apply_rotation(
        query_proj.reshape(tok_rows, query_heads, head_dim), token_positions
    ).astype(jnp.bfloat16)
    rotated_keys = apply_rotation(
        key_projected.reshape(tok_rows, kv_heads, head_dim), token_positions
    ).astype(jnp.bfloat16)
    fresh_values = value_projected.astype(jnp.bfloat16)
    q_local = rotated_queries.reshape(
        query_blocks, block_len, kv_heads, query_group_width, head_dim
    )
    k_local = rotated_keys.reshape(query_blocks, block_len, kv_heads, head_dim)
    v_local = fresh_values.reshape(query_blocks, block_len, kv_heads, head_dim)
    mixed = attend(q_local, selected, selected_alive_mask, k_local, v_local)
    return mixed.astype(jnp.bfloat16).reshape(tok_rows, query_heads * head_dim)


def swap(values, mask):
    pairs = [(i, i ^ mask) for i in range(lax.axis_size("ctx"))]
    return lax.ppermute(values, "ctx", pairs)


def project_kernel(rotated, order, *refs):
    own, other, pieces = refs[0:4], refs[4:8], refs[8:16]
    cosine, sine, out, total, piece = refs[16:]
    step = pl.program_id(0)
    rows = own[0].shape[0]

    @pl.when(step == 0)
    def _():
        total[...] = jnp.zeros_like(total)

    for number in range(8):

        @pl.when(step == number)
        def _(number=number):
            piece[...] = pieces[number][...]

    def add(parts):
        for number in range(4):
            total[pl.ds(number * rows, rows), :] += jnp.dot(
                parts[number][...], piece[...], preferred_element_type=jnp.float32
            )

    @pl.when(order[16 + step] == 1)
    def _():
        add(own)

    @pl.when(order[16 + step] == 0)
    def _():
        add(other)

    @pl.when(step == 7)
    def _():
        for number, turn in enumerate(rotated):
            columns = pl.ds(number * 128, 128)
            value = total[:, columns]
            if turn:
                value = value * cosine[...] + pltpu.roll(value, 64, 1) * sine[...]
            out[:, columns] = value.astype(out.dtype)


def project(order, own, other, pieces, cosine, sine, rotated):
    rows, depth, width = own[0].shape[0], pieces[0].shape[0], pieces[0].shape[1]
    whole = lambda shape: pl.BlockSpec(shape, lambda s, o: (0, 0))
    return pl.pallas_call(
        functools.partial(project_kernel, rotated),
        out_shape=jax.ShapeDtypeStruct((4 * rows, width), jnp.bfloat16),
        grid_spec=pltpu.PrefetchScalarGridSpec(
            num_scalar_prefetch=1,
            grid=(8,),
            in_specs=[pl.BlockSpec((rows, depth), lambda s, o: (0, o[s]))] * 4
            + [pl.BlockSpec((rows, depth), lambda s, o: (0, o[8 + s]))] * 4
            + [whole((depth, width))] * 8
            + [whole(cosine.shape)] * 2,
            out_specs=whole((4 * rows, width)),
            scratch_shapes=[
                pltpu.VMEM((4 * rows, width), jnp.float32),
                pltpu.VMEM((depth, width), jnp.bfloat16),
            ],
        ),
        compiler_params=pltpu.CompilerParams(vmem_limit_bytes=48 * 1024 * 1024),
        cost_estimate=pl.CostEstimate(
            flops=2 * 4 * rows * 8 * depth * width,
            bytes_accessed=2 * 4 * rows * 8 * depth + 2 * 8 * depth * width,
            transcendentals=0,
        ),
    )(order, *own, *other, *pieces, cosine, sine)


def attend_kernel(chosen, alive, query, fresh, cache, out):
    block = pl.program_id(0)
    tokens, heads, slots = query.shape[0], query.shape[1] // 128, 8
    scaling = 1.4426950408889634 / 128.0**0.5
    stacked = jnp.concatenate([query[:, pl.ds(h * 128, 128)] for h in range(heads)], axis=0)
    places = [chosen[block * slots + s] for s in range(slots)]
    keys = jnp.concatenate([cache[p, 0] for p in places] + [fresh[:, pl.ds(0, 128)]], axis=0)
    values = jnp.concatenate([cache[p, 1] for p in places] + [fresh[:, pl.ds(128, 128)]], axis=0)
    scores = lax.dot_general(
        stacked, keys, (((1,), (1,)), ((), ())), preferred_element_type=jnp.float32
    )
    parts = [
        jnp.where(alive[block * slots + s] > 0, scores[:, s * 128 : (s + 1) * 128], neg_fill)
        for s in range(slots)
    ]
    row = lax.rem(lax.broadcasted_iota(jnp.int32, (heads * tokens, tokens), 0), tokens)
    column = lax.broadcasted_iota(jnp.int32, (heads * tokens, tokens), 1)
    parts.append(jnp.where(row >= column, scores[:, slots * 128 :], neg_fill))
    top = jnp.max(functools.reduce(jnp.maximum, parts), axis=1, keepdims=True) * scaling
    weights = [jnp.exp2(part * scaling - top) for part in parts]
    total = jnp.sum(functools.reduce(jnp.add, weights), axis=1, keepdims=True)
    probs = jnp.concatenate([w.astype(jnp.bfloat16) for w in weights], axis=1)
    mixed = jnp.dot(probs, values, preferred_element_type=jnp.float32) / total
    for h in range(heads):
        out[:, pl.ds(h * 128, 128)] = mixed[h * tokens : (h + 1) * tokens].astype(out.dtype)


def attend_chunk(chosen, alive, query, fresh, cache):
    rows, width = query.shape
    blocks = rows // 128
    heads = width // 128
    return pl.pallas_call(
        attend_kernel,
        out_shape=jax.ShapeDtypeStruct((rows, width), jnp.bfloat16),
        grid_spec=pltpu.PrefetchScalarGridSpec(
            num_scalar_prefetch=2,
            grid=(blocks,),
            in_specs=[
                pl.BlockSpec((128, width), lambda b, c, a: (b, 0)),
                pl.BlockSpec((128, 256), lambda b, c, a: (b, 0)),
                pl.BlockSpec(cache.shape, lambda b, c, a: (0, 0, 0, 0)),
            ],
            out_specs=pl.BlockSpec((128, width), lambda b, c, a: (b, 0)),
        ),
        compiler_params=pltpu.CompilerParams(vmem_limit_bytes=48 * 1024 * 1024),
        cost_estimate=pl.CostEstimate(
            flops=4 * rows * heads * 1152 * 128 * 2,
            bytes_accessed=cache.size * 2 + rows * width * 4,
            transcendentals=rows * heads * 1152,
        ),
    )(chosen, alive, query, fresh, cache)


def grouped(
    tokens,
    w_query,
    key_weight,
    value_weight,
    prefix_cache_blocks,
    selected_owner,
    selected_offset,
    selected_alive_mask,
):
    rows, half = tokens.shape
    heads, blocks_dev, _, block_len, head_dim = prefix_cache_blocks.shape
    query_blocks, selections = selected_owner.shape[1:]
    ctx_devices = lax.axis_size("ctx")
    me = lax.axis_index("ctx")
    x, y, z = me & 1, (me >> 1) & 1, me >> 2
    low = z & 1
    mine = 2 * low + x
    group = (0, 1, 4, 5)
    chunks = 4
    width = w_query.shape[1] // heads // chunks

    def pick(values, index):
        return lax.dynamic_index_in_dim(values, index, 0, keepdims=False)

    def route(by_head):
        by_head = by_head.reshape((2, 2) + by_head.shape[1:])
        kept = lax.dynamic_index_in_dim(by_head, x, 1, keepdims=False)
        got = swap(lax.dynamic_index_in_dim(by_head, 1 - x, 1, keepdims=False), 1)

        def joined(index):
            one, two = pick(kept, index), pick(got, index)
            return jnp.concatenate([jnp.where(x == 0, one, two), jnp.where(x == 0, two, one)], axis=0)

        here, there = joined(low), joined(1 - low)
        planes = [here, swap(there, 4), swap(here, 8), swap(there, 12)]
        return [piece for plane in planes for piece in (plane, swap(plane, 2))]

    by_head = w_query.reshape(rows, heads, chunks, width).transpose(1, 2, 0, 3)
    fresh_weight = jnp.concatenate(
        [key_weight.reshape(rows, heads, head_dim), value_weight.reshape(rows, heads, head_dim)], axis=2
    ).transpose(1, 0, 2)

    over_x, over_z = swap(tokens, 1), swap(tokens, 4)
    own = [tokens, over_x, over_z, swap(over_z, 1)]
    other = [lax.ppermute(t, "tp", [(0, 1), (1, 0)]) for t in own]

    fresh_pieces = route(fresh_weight)
    cache = jnp.concatenate(route(prefix_cache_blocks), axis=0)
    query_pieces = [route(by_head[:, c]) for c in range(chunks)]

    codes = (selected_owner * blocks_dev + selected_offset) * 2 + selected_alive_mask
    codes = jnp.stack([pick(codes, mine)] + [swap(pick(codes, mine ^ m), (0, 1, 4, 5)[m]) for m in (1, 2, 3)])
    codes = codes.reshape(-1)
    alive = codes & 1
    offset = (codes >> 1) % blocks_dev
    owner = (codes >> 1) // blocks_dev
    piece = ((owner >> 2) ^ z) * 2 + (((owner >> 1) & 1) ^ y)
    chosen = (piece * 2 + (owner & 1)) * blocks_dev + offset

    start = blocks_dev * ctx_devices * block_len
    positions = jnp.concatenate(
        [start + (me ^ m) * rows + jnp.arange(rows, dtype=jnp.int32) for m in group]
    )
    steps = jnp.arange(head_dim // 2).astype(jnp.float32)
    inverse = jnp.power(jnp.float32(rope_base), -2.0 * steps / head_dim)
    angle = positions.astype(jnp.float32)[:, None] * inverse[None, :]
    cosine, sine = jnp.cos(angle), jnp.sin(angle)
    cosine = jnp.concatenate([cosine, cosine], axis=1)
    sine = jnp.concatenate([-sine, sine], axis=1)

    place = jnp.arange(8, dtype=jnp.int32)
    column = (((place >> 1) ^ z) * 2 + ((place & 1) ^ y)) & 3
    early, late = column[jnp.minimum(place, 3)], column[jnp.maximum(place, 4)]
    own_first = lax.axis_index("tp") == (z >> 1)
    order = jnp.concatenate(
        [
            jnp.where(own_first, early, late),
            jnp.where(own_first, late, early),
            ((place < 4) == own_first).astype(jnp.int32),
        ]
    )

    fresh = project(order, own, other, fresh_pieces, cosine, sine, (True, False))
    out = jnp.zeros((rows, heads * chunks * width), tokens.dtype)
    for c in range(chunks):
        query = project(order, own, other, query_pieces[c], cosine, sine, (True,) * (width // head_dim))
        mixed = attend_chunk(chosen, alive, query, fresh, cache).reshape(4, rows, width)
        for m in range(4):
            part = swap(mixed[m], group[m]) if m else mixed[0]
            out = lax.dynamic_update_slice(out, part, (0, ((mine ^ m) * chunks + c) * width))
    return out


def solution(mesh):
    def per_shard(*args):
        tokens, w_query, cache = args[0], args[1], args[4]
        fits = (
            mesh.shape["ctx"] == 16
            and mesh.shape["tp"] == 2
            and cache.shape[0] == 4
            and cache.shape[3] == 128
            and cache.shape[4] == 128
            and w_query.shape[1] == 4096
            and tokens.shape == (512, 4096)
            and args[5].shape[2] == 8
        )
        return grouped(*args) if fits else per_device(*args)

    return jax.shard_map(
        per_shard,
        mesh=mesh,
        in_specs=(
            P("ctx", "tp"),
            P("ctx", "tp"),
            P("ctx", "tp"),
            P("ctx", "tp"),
            P("tp", "ctx", None, None, None),
            P("tp", "ctx", None),
            P("tp", "ctx", None),
            P("tp", "ctx", None),
        ),
        out_specs=P("ctx", "tp"),
        check_vma=False,
    )
```

```python
import functools

import jax
import jax.numpy as jnp
from jax import lax
from jax.experimental import pallas as pl
from jax.experimental.pallas import tpu as pltpu
from jax.sharding import PartitionSpec as P

rope_base = 500000.0
neg_fill = -1e30


def apply_rotation(values, token_positions):
    half_dim = values.shape[-1] // 2
    steps = jnp.arange(half_dim).astype(jnp.float32)
    inverse = jnp.power(jnp.float32(rope_base), -2.0 * steps / values.shape[-1])
    angle = token_positions.astype(jnp.float32)[:, None] * inverse[None, :]
    cosine = jnp.cos(angle)[:, None, :]
    sine_part = jnp.sin(angle)[:, None, :]
    lower_half = values[..., :half_dim]
    upper_half = values[..., half_dim:]
    return jnp.concatenate(
        [
            lower_half * cosine - upper_half * sine_part,
            upper_half * cosine + lower_half * sine_part,
        ],
        axis=-1,
    )


def attend(query, selected, live_slots, own_keys, own_values):
    scaling = 1.0 / jnp.sqrt(jnp.float32(query.shape[-1]))
    far_scores = (
        jnp.einsum(
            "bihgd,hbskd->bhgisk", query, selected[:, :, :, 0], preferred_element_type=jnp.float32
        )
        * scaling
    )
    alive = jnp.transpose(live_slots, (1, 0, 2))[:, :, None, None, :, None] > 0
    far_scores = jnp.where(alive, far_scores, neg_fill)
    near_scores = (
        jnp.einsum("bihgd,bjhd->bhgij", query, own_keys, preferred_element_type=jnp.float32)
        * scaling
    )
    row_ids = jnp.arange(query.shape[1])
    causal = row_ids[:, None] >= row_ids[None, :]
    near_scores = jnp.where(causal, near_scores, neg_fill)
    row_max = jnp.maximum(jnp.max(far_scores, axis=(4, 5)), jnp.max(near_scores, axis=4))
    far_exp = jnp.exp(far_scores - row_max[..., None, None])
    near_exp = jnp.exp(near_scores - row_max[..., None])
    denominator = jnp.sum(far_exp, axis=(4, 5)) + jnp.sum(near_exp, axis=4)
    far_prob = (far_exp / denominator[..., None, None]).astype(jnp.bfloat16)
    near_prob = (near_exp / denominator[..., None]).astype(jnp.bfloat16)
    mixed = jnp.einsum(
        "bhgisk,hbskd->bihgd", far_prob, selected[:, :, :, 1], preferred_element_type=jnp.float32
    )
    mixed = mixed + jnp.einsum(
        "bhgij,bjhd->bihgd", near_prob, own_values, preferred_element_type=jnp.float32
    )
    return mixed


def per_device(
    tokens,
    w_query,
    key_weight,
    value_weight,
    prefix_cache_blocks,
    selected_owner,
    selected_offset,
    selected_alive_mask,
):
    tok_rows = tokens.shape[0]
    ctx_devices = lax.axis_size("ctx")
    kv_heads = prefix_cache_blocks.shape[0]
    blocks_dev = prefix_cache_blocks.shape[1]
    block_len = prefix_cache_blocks.shape[3]
    head_dim = prefix_cache_blocks.shape[4]
    query_blocks = selected_owner.shape[1]
    selections = selected_owner.shape[2]
    query_heads = w_query.shape[1] // head_dim
    query_group_width = query_heads // kv_heads
    capacity = min(query_blocks, (query_blocks * selections + ctx_devices - 1) // ctx_devices + 1)
    gathered = lax.all_gather(tokens, "tp", axis=1, tiled=True)
    pieces = (
        lax.all_gather(w_query, "ctx", axis=0, tiled=True),
        lax.all_gather(key_weight, "ctx", axis=0, tiled=True),
        lax.all_gather(value_weight, "ctx", axis=0, tiled=True),
    )
    query_proj, key_projected, value_projected = tuple(
        (jnp.dot(gathered, shard_rows, preferred_element_type=jnp.float32) for shard_rows in pieces)
    )
    requests = query_blocks * selections
    owners = selected_owner.reshape(kv_heads, requests)
    offsets = selected_offset.reshape(kv_heads, requests)
    owner_hot = (owners[:, :, None] == jnp.arange(ctx_devices, dtype=jnp.int32)).astype(jnp.int32)
    earlier = jnp.cumsum(owner_hot, axis=1) - owner_hot
    ordinal = jnp.sum(earlier * owner_hot, axis=2)
    slot_count = kv_heads * capacity
    slot_index = jnp.arange(kv_heads, dtype=jnp.int32)[:, None] * capacity + ordinal
    slot_hot = (slot_index[:, :, None] == jnp.arange(slot_count, dtype=jnp.int32)).astype(jnp.int32)
    entries = jnp.arange(kv_heads, dtype=jnp.int32)[:, None] * blocks_dev + offsets
    outgoing = jnp.einsum("hrn,hrs->ns", owner_hot * entries[:, :, None], slot_hot)
    cache_table = prefix_cache_blocks.reshape(kv_heads * blocks_dev, 2, block_len, head_dim)
    found_blocks = jnp.take(
        cache_table,
        lax.all_to_all(outgoing, "ctx", split_axis=0, concat_axis=0, tiled=True),
        axis=0,
    )
    arrived = lax.all_to_all(found_blocks, "ctx", split_axis=0, concat_axis=0, tiled=True)
    flattened = arrived.reshape(ctx_devices * slot_count, 2, block_len, head_dim)
    locator = owners * slot_count + slot_index
    picked = jnp.take(flattened, locator.reshape(-1), axis=0)
    selected = picked.reshape(kv_heads, query_blocks, selections, 2, block_len, head_dim)
    token_positions = (
        blocks_dev * ctx_devices * block_len
        + lax.axis_index("ctx") * tok_rows
        + jnp.arange(tok_rows, dtype=jnp.int32)
    )
    rotated_queries = apply_rotation(
        query_proj.reshape(tok_rows, query_heads, head_dim), token_positions
    ).astype(jnp.bfloat16)
    rotated_keys = apply_rotation(
        key_projected.reshape(tok_rows, kv_heads, head_dim), token_positions
    ).astype(jnp.bfloat16)
    fresh_values = value_projected.astype(jnp.bfloat16)
    q_local = rotated_queries.reshape(
        query_blocks, block_len, kv_heads, query_group_width, head_dim
    )
    k_local = rotated_keys.reshape(query_blocks, block_len, kv_heads, head_dim)
    v_local = fresh_values.reshape(query_blocks, block_len, kv_heads, head_dim)
    mixed = attend(q_local, selected, selected_alive_mask, k_local, v_local)
    return mixed.astype(jnp.bfloat16).reshape(tok_rows, query_heads * head_dim)


def stage(done, *values):
    return lax.optimization_barrier(tuple(values) + tuple(done))[: len(values)]


def swap(values, mask):
    pairs = [(i, i ^ mask) for i in range(lax.axis_size("ctx"))]
    return lax.ppermute(values, "ctx", pairs)


def assemble_kernel(*refs):
    parts, out = refs[:-1], refs[-1]
    start = 0
    for part in parts:
        out[:, pl.ds(start, part.shape[1])] = part[...]
        start += part.shape[1]


def assemble(parts, rows):
    width = sum(part.shape[1] for part in parts)
    return pl.pallas_call(
        assemble_kernel,
        out_shape=jax.ShapeDtypeStruct((rows, 4 * width), parts[0].dtype),
        grid=(4,),
        in_specs=[pl.BlockSpec((rows, part.shape[1]), lambda k: (k, 0)) for part in parts],
        out_specs=pl.BlockSpec((rows, width), lambda k: (0, k)),
        compiler_params=pltpu.CompilerParams(vmem_limit_bytes=32 * 1024 * 1024),
    )(*parts)


def project_kernel(rotated, places, order, *refs):
    own, other, pieces, turns = refs[0:4], refs[4:8], refs[8:16], refs[16:18]
    out, total, columns, weights, tables, column_sems, weight_sems, table_sems = refs[18:]
    rows, width = own[0].shape[0], out.shape[1]
    depth, slots = 2 * rows, columns.shape[0]
    swapped = order[24]

    def column_copies(step, sources):
        start = pl.multiple_of(order[step] * depth, depth)
        return [
            pltpu.make_async_copy(
                sources[m].at[:, pl.ds(start, depth)],
                columns.at[step % slots, m],
                column_sems.at[step % slots, m],
            )
            for m in range(4)
        ]

    def weight_copies(step):
        row, column = places[step]
        return [
            pltpu.make_async_copy(
                pieces[step].at[pl.ds(row + h * rows, rows), pl.ds(column, width)],
                weights.at[step, pl.ds(pl.multiple_of((swapped ^ h) * rows, rows), rows), :],
                weight_sems.at[step, h],
            )
            for h in range(2)
        ]

    def start_columns(step):
        @pl.when(order[16 + step] == 1)
        def _():
            for copy in column_copies(step, own):
                copy.start()

        @pl.when(order[16 + step] == 0)
        def _():
            for copy in column_copies(step, other):
                copy.start()

    table_copies = [
        pltpu.make_async_copy(turn, tables.at[n], table_sems.at[n]) for n, turn in enumerate(turns)
    ]
    for step in range(8):
        if step < slots - 1:
            start_columns(step)
        for copy in weight_copies(step):
            copy.start()
    for copy in table_copies:
        copy.start()
    for step in range(8):
        if step + slots - 1 < 8:
            start_columns(step + slots - 1)
        for copy in column_copies(step, own) + weight_copies(step):
            copy.wait()
        for m in range(4):
            part = pl.ds(m * rows, rows)
            product = jnp.dot(
                columns[step % slots, m], weights[step], preferred_element_type=jnp.float32
            )
            if step:
                product += total[part, :]
            total[part, :] = product
    for copy in table_copies:
        copy.wait()
    for number, turn in enumerate(rotated):
        part = pl.ds(number * 128, 128)
        value = total[:, part]
        if turn:
            value = value * tables[0] + pltpu.roll(value, 64, 1) * tables[1]
        out[:, part] = value.astype(out.dtype)


def project(order, own, other, pieces, cosine, sine, rotated):
    rows, width = own[0].shape[0], 128 * len(rotated)
    depth, slots = 2 * rows, 3
    places = [place for _, place in pieces]
    return pl.pallas_call(
        functools.partial(project_kernel, rotated, places),
        out_shape=jax.ShapeDtypeStruct((4 * rows, width), jnp.bfloat16),
        grid_spec=pltpu.PrefetchScalarGridSpec(
            num_scalar_prefetch=1,
            grid=(1,),
            in_specs=[pl.BlockSpec(memory_space=pl.ANY)] * 18,
            out_specs=pl.BlockSpec((4 * rows, width), lambda s, o: (0, 0)),
            scratch_shapes=[
                pltpu.VMEM((4 * rows, width), jnp.float32),
                pltpu.VMEM((slots, 4, rows, depth), jnp.bfloat16),
                pltpu.VMEM((8, depth, width), jnp.bfloat16),
                pltpu.VMEM((2,) + cosine.shape, jnp.float32),
                pltpu.SemaphoreType.DMA((slots, 4)),
                pltpu.SemaphoreType.DMA((8, 2)),
                pltpu.SemaphoreType.DMA((2,)),
            ],
        ),
        compiler_params=pltpu.CompilerParams(vmem_limit_bytes=48 * 1024 * 1024),
        cost_estimate=pl.CostEstimate(
            flops=2 * 4 * rows * 8 * depth * width,
            bytes_accessed=2 * 4 * rows * 8 * depth + 2 * 8 * depth * width,
            transcendentals=0,
        ),
    )(order, *own, *other, *(array for array, _ in pieces), cosine, sine)


def attend_kernel(together, chosen, alive, query, fresh, *refs):
    sources, (out, cache, sems) = refs[:-3], refs[-3:]
    tokens, heads, slots = 128, query.shape[1] // 128, 8

    @pl.when(pl.program_id(0) == 0)
    def _():
        size = sources[0].shape[0]
        copies = [
            pltpu.make_async_copy(source, cache.at[pl.ds(n * size, size)], sems.at[n])
            for n, source in enumerate(sources)
        ]
        for copy in copies:
            copy.start()
        for copy in copies:
            copy.wait()

    scaling = 1.4426950408889634 / 128.0**0.5
    row = lax.broadcasted_iota(jnp.int32, (heads * tokens, tokens), 0) & (tokens - 1)
    column = lax.broadcasted_iota(jnp.int32, (heads * tokens, tokens), 1)
    causal = row >= column
    ones = jnp.where(lax.broadcasted_iota(jnp.int32, ((slots + 1) * 128, 128), 1) == 0, 1.0, 0.0)
    ones = ones.astype(jnp.bfloat16)
    for number in range(together):
        first = (pl.program_id(0) * together + number) * slots
        rows = pl.ds(number * tokens, tokens)
        places = [chosen[first + s] for s in range(slots)]
        stacked = jnp.concatenate([query[rows, pl.ds(h * 128, 128)] for h in range(heads)], axis=0)
        keys = [cache[p, 0] for p in places] + [fresh[rows, pl.ds(0, 128)]]
        values = [cache[p, 1] for p in places] + [fresh[rows, pl.ds(128, 128)]]
        values = jnp.concatenate([jnp.concatenate(values, axis=0), ones], axis=1)
        scores = lax.dot_general(
            stacked,
            jnp.concatenate(keys, axis=0),
            (((1,), (1,)), ((), ())),
            preferred_element_type=jnp.float32,
        )
        parts = [
            jnp.where(alive[first + s] > 0, scores[:, s * 128 : (s + 1) * 128], neg_fill)
            for s in range(slots)
        ]
        parts.append(jnp.where(causal, scores[:, slots * 128 :], neg_fill))
        top = jnp.max(functools.reduce(jnp.maximum, parts), axis=1, keepdims=True) * scaling
        weights = [jnp.exp2(part * scaling - top).astype(jnp.bfloat16) for part in parts]
        mixed = jnp.dot(
            jnp.concatenate(weights, axis=1), values, preferred_element_type=jnp.float32
        )
        mixed = mixed[:, :128] / mixed[:, 128:129]
        for h in range(heads):
            out[rows, pl.ds(h * 128, 128)] = mixed[h * tokens : (h + 1) * tokens].astype(out.dtype)


def attend_chunk(chosen, alive, mine, query, place, width, fresh, cache):
    rows, heads = query.shape[0], width // 128
    together = 4 if heads <= 2 else 2
    size = 128 * together
    flip = mine * (rows // size // 4)
    alive = jnp.concatenate([alive, flip[None]])
    return pl.pallas_call(
        functools.partial(attend_kernel, together),
        out_shape=jax.ShapeDtypeStruct((rows, width), jnp.bfloat16),
        grid_spec=pltpu.PrefetchScalarGridSpec(
            num_scalar_prefetch=2,
            grid=(rows // size,),
            in_specs=[
                pl.BlockSpec((size, width), lambda b, c, a: (b, place)),
                pl.BlockSpec((size, 256), lambda b, c, a: (b, 0)),
                *[pl.BlockSpec(memory_space=pl.ANY)] * len(cache),
            ],
            out_specs=pl.BlockSpec((size, width), lambda b, c, a: (b ^ a[rows // 128 * 8], 0)),
            scratch_shapes=[
                pltpu.VMEM((len(cache) * cache[0].shape[0],) + cache[0].shape[1:], cache[0].dtype),
                pltpu.SemaphoreType.DMA((len(cache),)),
            ],
        ),
        compiler_params=pltpu.CompilerParams(vmem_limit_bytes=48 * 1024 * 1024),
        cost_estimate=pl.CostEstimate(
            flops=16 * rows * heads * 1152 * 128,
            bytes_accessed=len(cache) * cache[0].size * 2 + rows * width * 4,
            transcendentals=rows * heads * 1152,
        ),
    )(chosen, alive, query, fresh, *cache)


def grouped(
    tokens,
    w_query,
    key_weight,
    value_weight,
    prefix_cache_blocks,
    selected_owner,
    selected_offset,
    selected_alive_mask,
):
    rows = tokens.shape[0]
    heads, blocks_dev, _, block_len, head_dim = prefix_cache_blocks.shape
    query_blocks, selections = selected_owner.shape[1:]
    ctx_devices = lax.axis_size("ctx")
    me = lax.axis_index("ctx")
    x, y, z = me & 1, (me >> 1) & 1, me >> 2
    mine = 2 * (z & 1) + x
    group = (0, 1, 4, 5)
    per_head = w_query.shape[1] // heads
    chunks = ((True, 0, 2), (False, 2, 4), (False, 6, 2))
    along_x, along_y, along_z = 1, 2, 4
    lines = [[i + 4 * q for q in range(4)] for i in range(4)]

    def columns(chunk):
        with_fresh, first, count = chunk

        def of_head(k):
            start = k * per_head + first * head_dim
            part = lax.dynamic_slice(w_query, (0, start), (rows, count * head_dim))
            if with_fresh:
                fresh = [
                    lax.dynamic_slice(w, (0, k * head_dim), (rows, head_dim))
                    for w in (key_weight, value_weight)
                ]
                part = jnp.concatenate(fresh + [part], axis=1)
            return part

        return of_head

    def cached(k):
        return lax.dynamic_index_in_dim(prefix_cache_blocks, k, 0, keepdims=False)

    def given(of_head):
        return jnp.concatenate([of_head(1 - x), of_head(3 - x)], axis=0)

    def joined(of_head, got):
        even, odd = jnp.split(got, 2, axis=0)
        even = jnp.concatenate([of_head(x), even], axis=0)
        odd = jnp.concatenate([of_head(2 + x), odd], axis=0)
        return even, odd

    def over_z(even_odd_twice, *beside):
        planes = lax.all_to_all(even_odd_twice, "ctx", 0, 0, axis_index_groups=lines, tiled=True)
        return stage(beside, planes)[0] if beside else planes

    def twice(even, odd):
        return jnp.concatenate([even, odd, even, odd], axis=0)

    def over_tp(values):
        return lax.ppermute(values, "tp", [(0, 1), (1, 0)])

    def listed(planes, planes_y):
        return [(array, (q * 2 * rows, 0)) for q in range(4) for array in (planes, planes_y)]

    start = blocks_dev * ctx_devices * block_len
    positions = jnp.concatenate(
        [start + (me ^ m) * rows + jnp.arange(rows, dtype=jnp.int32) for m in group]
    )
    steps = jnp.arange(head_dim // 2).astype(jnp.float32)
    inverse = jnp.power(jnp.float32(rope_base), -2.0 * steps / head_dim)
    angle = positions.astype(jnp.float32)[:, None] * inverse[None, :]
    cosine, sine = jnp.cos(angle), jnp.sin(angle)
    cosine = jnp.concatenate([cosine, cosine], axis=1)
    sine = jnp.concatenate([-sine, sine], axis=1)

    q_0, q_1, q_2, q_3 = jnp.split(tokens, 4, axis=0)
    late_chunk = (False, 2, 6)
    a_got = swap(given(columns(chunks[0])), along_x)
    z_0 = swap(q_0, along_z)
    tokens_other = over_tp(tokens)

    sends = (twice(*joined(columns(chunks[0]), a_got)), given(cached), given(columns(late_chunk)), q_0, q_1)
    sends = stage((a_got, z_0, tokens_other), *sends)
    a_planes = over_z(sends[0])
    cache_got, late_got, x_0 = (swap(s, along_x) for s in sends[1:4])
    z_1 = swap(sends[4], along_z)

    late_even, late_odd = joined(columns(late_chunk), late_got)

    def late_twice(c):
        first = (chunks[c][1] - late_chunk[1]) * head_dim
        part = slice(first, first + chunks[c][2] * head_dim)
        return twice(late_even[:, part], late_odd[:, part])

    sends = (twice(*joined(cached, cache_got)), q_1, q_2, q_3, z_0, z_1, q_2, q_3, a_planes)
    sends = stage((a_planes, cache_got, late_got, x_0, z_1), *sends)
    cache_planes = over_z(sends[0])
    x_1, x_2, x_3, xz_0, xz_1 = (swap(s, along_x) for s in sends[1:6])
    z_2, z_3 = (swap(s, along_z) for s in sends[6:8])
    a_planes_y = swap(sends[8], along_y)

    tokens_x = jnp.concatenate([x_0, x_1, x_2, x_3], axis=0)
    sends = (late_twice(1), z_2, z_3, cache_planes, tokens_x)
    done = (cache_planes, x_1, x_2, x_3, xz_0, xz_1, z_2, z_3, a_planes_y, cosine, sine)
    sends = stage(done, *sends)
    b_planes = over_z(sends[0])
    xz_2, xz_3 = (swap(s, along_x) for s in sends[1:3])
    cache_planes_y = swap(sends[3], along_y)
    tokens_x_other = over_tp(sends[4])
    codes = (selected_owner * blocks_dev + selected_offset) * 2 + selected_alive_mask
    code = lambda m: lax.dynamic_index_in_dim(codes, mine ^ m, 0, keepdims=False)
    codes = [code(0)] + [swap(code(m), group[m]) for m in (1, 2, 3)]

    tokens_z = jnp.concatenate([z_0, z_1, z_2, z_3], axis=0)
    tokens_xz = jnp.concatenate([xz_0, xz_1, xz_2, xz_3], axis=0)
    sends = (late_twice(2), b_planes, tokens_z, tokens_xz)
    done = (b_planes, xz_2, xz_3, cache_planes_y, tokens_x_other, *codes[1:])
    sends = stage(done, *sends)
    c_send = sends[0]
    b_planes_y = swap(sends[1], along_y)
    tokens_z_other, tokens_xz_other = (over_tp(s) for s in sends[2:])
    own = [tokens, tokens_x, tokens_z, tokens_xz]
    other = [tokens_other, tokens_x_other, tokens_z_other, tokens_xz_other]
    cache = (cache_planes, cache_planes_y)

    codes = jnp.stack(codes).reshape(-1)
    alive = codes & 1
    offset = (codes >> 1) % blocks_dev
    owner = (codes >> 1) // blocks_dev
    piece = (((owner >> 1) & 1) ^ y) * 4 + (owner >> 2)
    chosen = (piece * 2 + ((owner & 1) ^ x)) * blocks_dev + offset

    place = jnp.arange(8, dtype=jnp.int32)
    column = ((place >> 1) * 2 + ((place & 1) ^ y)) & 3
    own_first = lax.axis_index("tp") == 0
    order = jnp.concatenate(
        [column, column, ((place < 4) == own_first).astype(jnp.int32), x[None]]
    )

    out = jnp.zeros((rows, heads * per_head), tokens.dtype)
    fresh = None

    def compute(chunk, *pieces):
        with_fresh, first, count = chunk
        turned = (True, False) * with_fresh + (True,) * count
        query = project(order, own, other, pieces, cosine, sine, turned)
        width = count * head_dim
        mixed = attend_chunk(
            chosen, alive, mine, query, int(with_fresh), width, query if with_fresh else fresh, cache
        )
        return query, mixed

    squares = [[8 * p + 2 * q + m for m in group] for p in range(2) for q in range(2)]

    def home(mixed):
        return lax.all_to_all(mixed, "ctx", 0, 0, axis_index_groups=squares, tiled=True)

    fresh, a_mixed = compute(chunks[0], *listed(a_planes, a_planes_y))
    c_planes = over_z(c_send, a_mixed)
    (send,) = stage((c_planes, b_planes_y, a_mixed), c_planes)
    c_planes_y = swap(send, along_y)
    a_out = home(a_mixed)
    _, b_mixed = compute(chunks[1], *listed(b_planes, b_planes_y))
    (c_planes,) = stage((b_mixed, a_out), c_planes)
    b_out = home(b_mixed)
    _, c_mixed = compute(chunks[2], *listed(c_planes, c_planes_y))
    return assemble([a_out, b_out, home(c_mixed)], rows)


def solution(mesh):
    def per_shard(*args):
        tokens, w_query, cache = args[0], args[1], args[4]
        fits = (
            mesh.shape["ctx"] == 16
            and mesh.shape["tp"] == 2
            and cache.shape[0] == 4
            and cache.shape[3] == 128
            and cache.shape[4] == 128
            and w_query.shape[1] == 4096
            and tokens.shape == (512, 4096)
            and args[5].shape[2] == 8
        )
        return grouped(*args) if fits else per_device(*args)

    return jax.shard_map(
        per_shard,
        mesh=mesh,
        in_specs=(
            P("ctx", "tp"),
            P("ctx", "tp"),
            P("ctx", "tp"),
            P("ctx", "tp"),
            P("tp", "ctx", None, None, None),
            P("tp", "ctx", None),
            P("tp", "ctx", None),
            P("tp", "ctx", None),
        ),
        out_specs=P("ctx", "tp"),
        check_vma=False,
    )
```

```python
import functools

import jax
import jax.numpy as jnp
from jax import lax
from jax.experimental import pallas as pl
from jax.experimental.pallas import tpu as pltpu
from jax.sharding import PartitionSpec as P

rope_base = 500000.0
neg_fill = -1e30


def apply_rotation(values, token_positions):
    half_dim = values.shape[-1] // 2
    steps = jnp.arange(half_dim).astype(jnp.float32)
    inverse = jnp.power(jnp.float32(rope_base), -2.0 * steps / values.shape[-1])
    angle = token_positions.astype(jnp.float32)[:, None] * inverse[None, :]
    cosine = jnp.cos(angle)[:, None, :]
    sine_part = jnp.sin(angle)[:, None, :]
    lower_half = values[..., :half_dim]
    upper_half = values[..., half_dim:]
    return jnp.concatenate(
        [
            lower_half * cosine - upper_half * sine_part,
            upper_half * cosine + lower_half * sine_part,
        ],
        axis=-1,
    )


def attend(query, selected, live_slots, own_keys, own_values):
    scaling = 1.0 / jnp.sqrt(jnp.float32(query.shape[-1]))
    far_scores = (
        jnp.einsum(
            "bihgd,hbskd->bhgisk", query, selected[:, :, :, 0], preferred_element_type=jnp.float32
        )
        * scaling
    )
    alive = jnp.transpose(live_slots, (1, 0, 2))[:, :, None, None, :, None] > 0
    far_scores = jnp.where(alive, far_scores, neg_fill)
    near_scores = (
        jnp.einsum("bihgd,bjhd->bhgij", query, own_keys, preferred_element_type=jnp.float32)
        * scaling
    )
    row_ids = jnp.arange(query.shape[1])
    causal = row_ids[:, None] >= row_ids[None, :]
    near_scores = jnp.where(causal, near_scores, neg_fill)
    row_max = jnp.maximum(jnp.max(far_scores, axis=(4, 5)), jnp.max(near_scores, axis=4))
    far_exp = jnp.exp(far_scores - row_max[..., None, None])
    near_exp = jnp.exp(near_scores - row_max[..., None])
    denominator = jnp.sum(far_exp, axis=(4, 5)) + jnp.sum(near_exp, axis=4)
    far_prob = (far_exp / denominator[..., None, None]).astype(jnp.bfloat16)
    near_prob = (near_exp / denominator[..., None]).astype(jnp.bfloat16)
    mixed = jnp.einsum(
        "bhgisk,hbskd->bihgd", far_prob, selected[:, :, :, 1], preferred_element_type=jnp.float32
    )
    mixed = mixed + jnp.einsum(
        "bhgij,bjhd->bihgd", near_prob, own_values, preferred_element_type=jnp.float32
    )
    return mixed


def per_device(
    tokens,
    w_query,
    key_weight,
    value_weight,
    prefix_cache_blocks,
    selected_owner,
    selected_offset,
    selected_alive_mask,
):
    tok_rows = tokens.shape[0]
    ctx_devices = lax.axis_size("ctx")
    kv_heads = prefix_cache_blocks.shape[0]
    blocks_dev = prefix_cache_blocks.shape[1]
    block_len = prefix_cache_blocks.shape[3]
    head_dim = prefix_cache_blocks.shape[4]
    query_blocks = selected_owner.shape[1]
    selections = selected_owner.shape[2]
    query_heads = w_query.shape[1] // head_dim
    query_group_width = query_heads // kv_heads
    capacity = min(query_blocks, (query_blocks * selections + ctx_devices - 1) // ctx_devices + 1)
    gathered = lax.all_gather(tokens, "tp", axis=1, tiled=True)
    pieces = (
        lax.all_gather(w_query, "ctx", axis=0, tiled=True),
        lax.all_gather(key_weight, "ctx", axis=0, tiled=True),
        lax.all_gather(value_weight, "ctx", axis=0, tiled=True),
    )
    query_proj, key_projected, value_projected = tuple(
        (jnp.dot(gathered, shard_rows, preferred_element_type=jnp.float32) for shard_rows in pieces)
    )
    requests = query_blocks * selections
    owners = selected_owner.reshape(kv_heads, requests)
    offsets = selected_offset.reshape(kv_heads, requests)
    owner_hot = (owners[:, :, None] == jnp.arange(ctx_devices, dtype=jnp.int32)).astype(jnp.int32)
    earlier = jnp.cumsum(owner_hot, axis=1) - owner_hot
    ordinal = jnp.sum(earlier * owner_hot, axis=2)
    slot_count = kv_heads * capacity
    slot_index = jnp.arange(kv_heads, dtype=jnp.int32)[:, None] * capacity + ordinal
    slot_hot = (slot_index[:, :, None] == jnp.arange(slot_count, dtype=jnp.int32)).astype(jnp.int32)
    entries = jnp.arange(kv_heads, dtype=jnp.int32)[:, None] * blocks_dev + offsets
    outgoing = jnp.einsum("hrn,hrs->ns", owner_hot * entries[:, :, None], slot_hot)
    cache_table = prefix_cache_blocks.reshape(kv_heads * blocks_dev, 2, block_len, head_dim)
    found_blocks = jnp.take(
        cache_table,
        lax.all_to_all(outgoing, "ctx", split_axis=0, concat_axis=0, tiled=True),
        axis=0,
    )
    arrived = lax.all_to_all(found_blocks, "ctx", split_axis=0, concat_axis=0, tiled=True)
    flattened = arrived.reshape(ctx_devices * slot_count, 2, block_len, head_dim)
    locator = owners * slot_count + slot_index
    picked = jnp.take(flattened, locator.reshape(-1), axis=0)
    selected = picked.reshape(kv_heads, query_blocks, selections, 2, block_len, head_dim)
    token_positions = (
        blocks_dev * ctx_devices * block_len
        + lax.axis_index("ctx") * tok_rows
        + jnp.arange(tok_rows, dtype=jnp.int32)
    )
    rotated_queries = apply_rotation(
        query_proj.reshape(tok_rows, query_heads, head_dim), token_positions
    ).astype(jnp.bfloat16)
    rotated_keys = apply_rotation(
        key_projected.reshape(tok_rows, kv_heads, head_dim), token_positions
    ).astype(jnp.bfloat16)
    fresh_values = value_projected.astype(jnp.bfloat16)
    q_local = rotated_queries.reshape(
        query_blocks, block_len, kv_heads, query_group_width, head_dim
    )
    k_local = rotated_keys.reshape(query_blocks, block_len, kv_heads, head_dim)
    v_local = fresh_values.reshape(query_blocks, block_len, kv_heads, head_dim)
    mixed = attend(q_local, selected, selected_alive_mask, k_local, v_local)
    return mixed.astype(jnp.bfloat16).reshape(tok_rows, query_heads * head_dim)


def stage(done, *values):
    return lax.optimization_barrier(tuple(values) + tuple(done))[: len(values)]


def swap(values, mask):
    pairs = [(i, i ^ mask) for i in range(lax.axis_size("ctx"))]
    return lax.ppermute(values, "ctx", pairs)


def copy_kernel(places, source, target):
    target[...] = source[...]


def take_planes(places, values, column, width):
    size = values.shape[0] // 4
    return pl.pallas_call(
        copy_kernel,
        out_shape=jax.ShapeDtypeStruct((3 * size, width), values.dtype),
        grid_spec=pltpu.PrefetchScalarGridSpec(
            num_scalar_prefetch=1,
            grid=(3,),
            in_specs=[pl.BlockSpec((size, width), lambda i, p: (p[i], column))],
            out_specs=pl.BlockSpec((size, width), lambda i, p: (i, 0)),
        ),
        compiler_params=pltpu.CompilerParams(vmem_limit_bytes=32 * 1024 * 1024),
    )(places, values)


def assemble_kernel(mine, *refs):
    parts, out = refs[:-1], refs[-1]
    for m in range(4):

        @pl.when(pl.program_id(0) == m)
        def _(m=m):
            start = 0
            for part in parts[m::4]:
                out[:, pl.ds(start, part.shape[1])] = part[...]
                start += part.shape[1]


def assemble(mine, chunks):
    parts = [part for chunk in chunks for part in chunk]
    rows, width = parts[0].shape[0], sum(chunk[0].shape[1] for chunk in chunks)
    return pl.pallas_call(
        assemble_kernel,
        out_shape=jax.ShapeDtypeStruct((rows, 4 * width), parts[0].dtype),
        grid_spec=pltpu.PrefetchScalarGridSpec(
            num_scalar_prefetch=1,
            grid=(4,),
            in_specs=[pl.BlockSpec(part.shape, lambda m, k: (0, 0)) for part in parts],
            out_specs=pl.BlockSpec((rows, width), lambda m, k: (0, m ^ k[0])),
        ),
        compiler_params=pltpu.CompilerParams(vmem_limit_bytes=32 * 1024 * 1024),
    )(mine[None], *parts)


def project_kernel(rotated, places, starts, order, *refs):
    count = len(starts)
    own, other, refs = refs[:count], refs[count : 2 * count], refs[2 * count :]
    pieces, turns = refs[:8], refs[8:10]
    out, total, columns, weights, tables, column_sems, weight_sems, table_sems = refs[10:]
    slots, depth, width = columns.shape[0], columns.shape[2], out.shape[1]
    rows = depth // 2
    swapped = order[24]

    def column_copies(step, sources):
        start = pl.multiple_of(order[step] * depth, depth)
        return [
            pltpu.make_async_copy(
                source.at[:, pl.ds(start, depth)],
                columns.at[step % slots, pl.ds(starts[n], source.shape[0]), :],
                column_sems.at[step % slots, n],
            )
            for n, source in enumerate(sources)
        ]

    def weight_copies(step):
        plane, row, column = places[step]
        if plane is not None:
            row = order[25 + plane] * depth
        return [
            pltpu.make_async_copy(
                pieces[step].at[pl.ds(pl.multiple_of(row + h * rows, rows), rows), pl.ds(column, width)],
                weights.at[step, pl.ds(pl.multiple_of((swapped ^ h) * rows, rows), rows), :],
                weight_sems.at[step, h],
            )
            for h in range(2)
        ]

    def start_columns(step):
        @pl.when(order[16 + step] == 1)
        def _():
            for copy in column_copies(step, own):
                copy.start()

        @pl.when(order[16 + step] == 0)
        def _():
            for copy in column_copies(step, other):
                copy.start()

    table_copies = [
        pltpu.make_async_copy(turn, tables.at[n], table_sems.at[n]) for n, turn in enumerate(turns)
    ]
    for step in range(8):
        if step < slots - 1:
            start_columns(step)
        for copy in weight_copies(step):
            copy.start()
    for copy in table_copies:
        copy.start()
    for step in range(8):
        if step + slots - 1 < 8:
            start_columns(step + slots - 1)
        for copy in column_copies(step, own) + weight_copies(step):
            copy.wait()
        for m in range(4):
            part = pl.ds(m * rows, rows)
            product = jnp.dot(
                columns[step % slots, part, :], weights[step], preferred_element_type=jnp.float32
            )
            if step:
                product += total[part, :]
            total[part, :] = product
    for copy in table_copies:
        copy.wait()
    for number, turn in enumerate(rotated):
        part = pl.ds(number * 128, 128)
        value = total[:, part]
        if turn:
            value = value * tables[0] + pltpu.roll(value, 64, 1) * tables[1]
        out[:, part] = value.astype(out.dtype)


def project(order, own, other, pieces, cosine, sine, rotated):
    rows, width = own[0].shape[0], 128 * len(rotated)
    depth, slots = 2 * rows, 3
    starts = [sum(part.shape[0] for part in own[:n]) for n in range(len(own))]
    places = [place for _, place in pieces]
    return pl.pallas_call(
        functools.partial(project_kernel, rotated, places, starts),
        out_shape=jax.ShapeDtypeStruct((4 * rows, width), jnp.bfloat16),
        grid_spec=pltpu.PrefetchScalarGridSpec(
            num_scalar_prefetch=1,
            grid=(1,),
            in_specs=[pl.BlockSpec(memory_space=pl.ANY)] * (2 * len(own) + 10),
            out_specs=pl.BlockSpec((4 * rows, width), lambda s, o: (0, 0)),
            scratch_shapes=[
                pltpu.VMEM((4 * rows, width), jnp.float32),
                pltpu.VMEM((slots, 4 * rows, depth), jnp.bfloat16),
                pltpu.VMEM((8, depth, width), jnp.bfloat16),
                pltpu.VMEM((2,) + cosine.shape, jnp.float32),
                pltpu.SemaphoreType.DMA((slots, len(own))),
                pltpu.SemaphoreType.DMA((8, 2)),
                pltpu.SemaphoreType.DMA((2,)),
            ],
        ),
        compiler_params=pltpu.CompilerParams(vmem_limit_bytes=48 * 1024 * 1024),
        cost_estimate=pl.CostEstimate(
            flops=2 * 4 * rows * 8 * depth * width,
            bytes_accessed=2 * 4 * rows * 8 * depth + 2 * 8 * depth * width,
            transcendentals=0,
        ),
    )(order, *own, *other, *(array for array, _ in pieces), cosine, sine)


def attend_kernel(together, chosen, alive, query, fresh, *refs):
    sources, (out, cache, sems) = refs[:-3], refs[-3:]
    tokens, heads, slots = 128, query.shape[1] // 128, 8

    @pl.when(pl.program_id(0) == 0)
    def _():
        size = sources[0].shape[0]
        copies = [
            pltpu.make_async_copy(source, cache.at[pl.ds(n * size, size)], sems.at[n])
            for n, source in enumerate(sources)
        ]
        for copy in copies:
            copy.start()
        for copy in copies:
            copy.wait()

    scaling = 1.4426950408889634 / 128.0**0.5
    row = lax.broadcasted_iota(jnp.int32, (heads * tokens, tokens), 0) & (tokens - 1)
    column = lax.broadcasted_iota(jnp.int32, (heads * tokens, tokens), 1)
    causal = row >= column
    ones = jnp.where(lax.broadcasted_iota(jnp.int32, ((slots + 1) * 128, 128), 1) == 0, 1.0, 0.0)
    ones = ones.astype(jnp.bfloat16)
    for number in range(together):
        first = (pl.program_id(0) * together + number) * slots
        rows = pl.ds(number * tokens, tokens)
        places = [chosen[first + s] for s in range(slots)]
        stacked = jnp.concatenate([query[rows, pl.ds(h * 128, 128)] for h in range(heads)], axis=0)
        keys = [cache[p, 0] for p in places] + [fresh[rows, pl.ds(0, 128)]]
        values = [cache[p, 1] for p in places] + [fresh[rows, pl.ds(128, 128)]]
        values = jnp.concatenate([jnp.concatenate(values, axis=0), ones], axis=1)
        scores = lax.dot_general(
            stacked,
            jnp.concatenate(keys, axis=0),
            (((1,), (1,)), ((), ())),
            preferred_element_type=jnp.float32,
        )
        parts = [
            jnp.where(alive[first + s] > 0, scores[:, s * 128 : (s + 1) * 128], neg_fill)
            for s in range(slots)
        ]
        parts.append(jnp.where(causal, scores[:, slots * 128 :], neg_fill))
        top = jnp.max(functools.reduce(jnp.maximum, parts), axis=1, keepdims=True) * scaling
        weights = [jnp.exp2(part * scaling - top).astype(jnp.bfloat16) for part in parts]
        mixed = jnp.dot(
            jnp.concatenate(weights, axis=1), values, preferred_element_type=jnp.float32
        )
        mixed = mixed[:, :128] / mixed[:, 128:129]
        for h in range(heads):
            out[rows, pl.ds(h * 128, 128)] = mixed[h * tokens : (h + 1) * tokens].astype(out.dtype)


def attend_chunk(chosen, alive, query, place, width, fresh, cache):
    rows, heads = query.shape[0], width // 128
    together = 4 if heads <= 2 else 2
    size = 128 * together
    return pl.pallas_call(
        functools.partial(attend_kernel, together),
        out_shape=jax.ShapeDtypeStruct((rows, width), jnp.bfloat16),
        grid_spec=pltpu.PrefetchScalarGridSpec(
            num_scalar_prefetch=2,
            grid=(rows // size,),
            in_specs=[
                pl.BlockSpec((size, width), lambda b, c, a: (b, place)),
                pl.BlockSpec((size, 256), lambda b, c, a: (b, 0)),
                *[pl.BlockSpec(memory_space=pl.ANY)] * len(cache),
            ],
            out_specs=pl.BlockSpec((size, width), lambda b, c, a: (b, 0)),
            scratch_shapes=[
                pltpu.VMEM((len(cache) * cache[0].shape[0],) + cache[0].shape[1:], cache[0].dtype),
                pltpu.SemaphoreType.DMA((len(cache),)),
            ],
        ),
        compiler_params=pltpu.CompilerParams(vmem_limit_bytes=48 * 1024 * 1024),
        cost_estimate=pl.CostEstimate(
            flops=16 * rows * heads * 1152 * 128,
            bytes_accessed=len(cache) * cache[0].size * 2 + rows * width * 4,
            transcendentals=rows * heads * 1152,
        ),
    )(chosen, alive, query, fresh, *cache)


def grouped(
    tokens,
    w_query,
    key_weight,
    value_weight,
    prefix_cache_blocks,
    selected_owner,
    selected_offset,
    selected_alive_mask,
):
    rows = tokens.shape[0]
    heads, blocks_dev, _, block_len, head_dim = prefix_cache_blocks.shape
    query_blocks, selections = selected_owner.shape[1:]
    ctx_devices = lax.axis_size("ctx")
    me = lax.axis_index("ctx")
    x, y, z = me & 1, (me >> 1) & 1, me >> 2
    mine = 2 * (z & 1) + x
    group = (0, 1, 4, 5)
    per_head = w_query.shape[1] // heads
    chunks = ((True, 0, 2), (False, 2, 2), (False, 4, 2), (False, 6, 2))
    along_x, along_y, along_z = 1, 2, 4
    lines = [[i + 4 * q for q in range(4)] for i in range(4)]

    def columns(chunk):
        with_fresh, first, count = chunk

        def of_head(k):
            start = k * per_head + first * head_dim
            part = lax.dynamic_slice(w_query, (0, start), (rows, count * head_dim))
            if with_fresh:
                fresh = [
                    lax.dynamic_slice(w, (0, k * head_dim), (rows, head_dim))
                    for w in (key_weight, value_weight)
                ]
                part = jnp.concatenate(fresh + [part], axis=1)
            return part

        return of_head

    def cached(k):
        return lax.dynamic_index_in_dim(prefix_cache_blocks, k, 0, keepdims=False)

    def given(of_head):
        return jnp.concatenate([of_head(1 - x), of_head(3 - x)], axis=0)

    def joined(of_head, got):
        even, odd = jnp.split(got, 2, axis=0)
        even = jnp.concatenate([of_head(x), even], axis=0)
        odd = jnp.concatenate([of_head(2 + x), odd], axis=0)
        return even, odd

    def over_z(even_odd_twice, *beside):
        planes = lax.all_to_all(even_odd_twice, "ctx", 0, 0, axis_index_groups=lines, tiled=True)
        return stage(beside, planes)[0] if beside else planes

    def twice(even, odd):
        return jnp.concatenate([even, odd, even, odd], axis=0)

    def over_tp(values):
        return lax.ppermute(values, "tp", [(0, 1), (1, 0)])

    def listed(planes, planes_y):
        return [(array, (r, 0, 0)) for r in range(4) for array in (planes, planes_y)]

    def late_listed(c, planes, column, others_y):
        pieces = [(planes, (0, 0, column)), (late_here_y, (None, 0, late_start(c)))]
        for r in (1, 2, 3):
            pieces += [(planes, (r, 0, column)), (others_y, (None, (r - 1) * 2 * rows, 0))]
        return pieces

    def others(planes, block=0):
        return take_planes(jnp.stack([z ^ 1, z ^ 2, z ^ 3]), planes, block, 256)

    start = blocks_dev * ctx_devices * block_len
    positions = jnp.concatenate(
        [start + (me ^ m) * rows + jnp.arange(rows, dtype=jnp.int32) for m in group]
    )
    steps = jnp.arange(head_dim // 2).astype(jnp.float32)
    inverse = jnp.power(jnp.float32(rope_base), -2.0 * steps / head_dim)
    angle = positions.astype(jnp.float32)[:, None] * inverse[None, :]
    cosine, sine = jnp.cos(angle), jnp.sin(angle)
    cosine = jnp.concatenate([cosine, cosine], axis=1)
    sine = jnp.concatenate([-sine, sine], axis=1)

    place = jnp.arange(8, dtype=jnp.int32)
    planes = (place >> 1) ^ z
    column = (planes * 2 + ((place & 1) ^ y)) & 3
    own_half = (planes >> 1) == lax.axis_index("tp")
    order = jnp.concatenate(
        [column, column, own_half.astype(jnp.int32), x[None], planes[::2]]
    )

    out = jnp.zeros((rows, heads * per_head), tokens.dtype)

    cut = rows * 5 // 16
    q_0, q_1, q_2 = tokens[:cut], tokens[cut : 2 * cut], tokens[2 * cut :]
    late_chunk = (False, 2, 6)
    a_got = swap(given(columns(chunks[0])), along_x)
    z_0 = swap(q_0, along_z)
    tokens_other = over_tp(tokens)
    codes = (selected_owner * blocks_dev + selected_offset) * 2 + selected_alive_mask
    code = lambda m: lax.dynamic_index_in_dim(codes, mine ^ m, 0, keepdims=False)
    codes = [code(0)] + [swap(code(m), group[m]) for m in (1, 2, 3)]

    sends = (twice(*joined(columns(chunks[0]), a_got)), given(cached), given(columns(late_chunk)), q_0, q_1)
    sends = stage((a_got, z_0, tokens_other), *sends)
    a_planes = over_z(sends[0])
    cache_got, late_got, x_0 = (swap(s, along_x) for s in sends[1:4])
    z_1 = swap(sends[4], along_z)

    late_even, late_odd = joined(columns(late_chunk), late_got)

    late_here_y = swap(jnp.where(z & 1 == 0, late_even, late_odd), along_y)

    def late_start(c):
        return (chunks[c][1] - late_chunk[1]) * head_dim

    def late_twice(c, count=1):
        part = slice(late_start(c), late_start(c) + count * 256)
        return twice(late_even[:, part], late_odd[:, part])

    sends = (twice(*joined(cached, cache_got)), q_1, q_2, z_0, q_2, a_planes, x_0, z_0, z_1)
    sends = stage((a_planes, cache_got, late_got, x_0, z_1, late_here_y, cosine, sine, *codes[1:]), *sends)
    cache_planes = over_z(sends[0])
    x_1, x_2, xz_0 = (swap(s, along_x) for s in sends[1:4])
    z_2 = swap(sends[4], along_z)
    a_planes_y = swap(sends[5], along_y)
    x_0o, z_0o, z_1o = (over_tp(s) for s in sends[6:])

    sends = (late_twice(1, 2), z_1, z_2, cache_planes, x_1, x_2, z_2, xz_0)
    sends = stage((cache_planes, x_1, x_2, xz_0, z_2, a_planes_y, x_0o, z_0o, z_1o), *sends)
    bc_planes = over_z(sends[0])
    xz_1, xz_2 = (swap(s, along_x) for s in sends[1:3])
    cache_planes_y = swap(sends[3], along_y)
    x_1o, x_2o, z_2o, xz_0o = (over_tp(s) for s in sends[4:])

    xz_1o, xz_2o = over_tp(xz_1), over_tp(xz_2)
    own = [tokens, x_0, x_1, x_2, z_0, z_1, z_2, xz_0, xz_1, xz_2]
    other = [tokens_other, x_0o, x_1o, x_2o, z_0o, z_1o, z_2o, xz_0o, xz_1o, xz_2o]
    fresh = project(order, own, other, listed(a_planes, a_planes_y), cosine, sine, (True, False, True, True))

    sends = (late_twice(3), others(bc_planes), bc_planes, fresh)
    d_send, send, bc_planes, fresh = stage((bc_planes, cache_planes_y, fresh), *sends)
    b_others_y = swap(send, along_y)
    c_others_y = swap(others(bc_planes, 1), along_y)
    cache = (cache_planes, cache_planes_y)

    codes = jnp.stack(codes).reshape(-1)
    alive = codes & 1
    offset = (codes >> 1) % blocks_dev
    owner = (codes >> 1) // blocks_dev
    piece = (((owner >> 1) & 1) ^ y) * 4 + (owner >> 2)
    chosen = (piece * 2 + ((owner & 1) ^ x)) * blocks_dev + offset

    def attend(query, place, width):
        return attend_chunk(chosen, alive, query, place, width, fresh, cache)

    def projected(chunk, pieces):
        return project(order, own, other, pieces, cosine, sine, (True,) * chunk[2])

    def home(mixed):
        mixed = mixed.reshape((4, rows) + mixed.shape[1:])
        return [mixed[0]] + [swap(mixed[m], group[m]) for m in (1, 2, 3)]

    a_mixed = attend(fresh, 1, 256)
    d_planes = over_z(d_send, a_mixed)
    (send,) = stage((d_planes, b_others_y, a_mixed), others(d_planes))
    d_others_y = swap(send, along_y)
    a_out = home(a_mixed)
    b_mixed = attend(projected(chunks[1], late_listed(1, bc_planes, 0, b_others_y)), 0, 256)
    b_out = home(b_mixed)
    (c_planes,) = stage((b_mixed, *a_out[1:]), bc_planes)
    c_mixed = attend(projected(chunks[2], late_listed(2, c_planes, 256, c_others_y)), 0, 256)
    c_out = home(c_mixed)
    (d_planes,) = stage((c_mixed, *b_out[1:]), d_planes)
    query = projected(chunks[3], late_listed(3, d_planes, 0, d_others_y))
    (query,) = stage(tuple(c_out[1:]), query)
    d_out = home(attend(query, 0, 256))
    return assemble(mine, [a_out, b_out, c_out, d_out])


def solution(mesh):
    def per_shard(*args):
        tokens, w_query, cache = args[0], args[1], args[4]
        fits = (
            mesh.shape["ctx"] == 16
            and mesh.shape["tp"] == 2
            and cache.shape[0] == 4
            and cache.shape[3] == 128
            and cache.shape[4] == 128
            and w_query.shape[1] == 4096
            and tokens.shape == (512, 4096)
            and args[5].shape[2] == 8
        )
        return grouped(*args) if fits else per_device(*args)

    return jax.shard_map(
        per_shard,
        mesh=mesh,
        in_specs=(
            P("ctx", "tp"),
            P("ctx", "tp"),
            P("ctx", "tp"),
            P("ctx", "tp"),
            P("tp", "ctx", None, None, None),
            P("tp", "ctx", None),
            P("tp", "ctx", None),
            P("tp", "ctx", None),
        ),
        out_specs=P("ctx", "tp"),
        check_vma=False,
    )
```
